32 devices in a mesh: dp: 32 (over z, y, x, core).
Axes of the slice: x: 2, y: 2, z: 4, core: 2. Of those that a mesh axis runs over, the one named last changes fastest.
Arguments:
- latents_in: bfloat16 [512, 256, 384], P('dp'), may hold values from -6 to 6
- class_ids: int32 [512], P('dp'), may hold values from 0 to 1000
- step_ids: int32 [512], P('dp'), may hold values from 0 to 999
- class_table: bfloat16 [1001, 384], replicated, may hold values from -4.1875 to 4.1875
- step_table: bfloat16 [1000, 384], replicated, may hold values from -4.1875 to 4.1875
- params: bfloat16 [2662400], P('dp'), may hold values from -1.5 to 1.5
- cotangent: bfloat16 [512, 256, 384], P('dp'), may hold values from -6 to 6
Outputs:
- block_out: bfloat16 [512, 256, 384], P('dp')
- grad_latents: bfloat16 [512, 256, 384], P('dp')
- grad_condition: float32 [512, 384], P('dp')
- grad_params: float32 [2662400], P('dp')
The draws below stay inside these ranges and needn't reach their ends.
All inputs are finite; a program needn't handle non-finite values.
Results may differ from the reference program's by a relative error of at most 0.012.
The reference program's roundings to bfloat16 on the way count: a program that leaves them out, or rounds other values in their place, can miss the bound.
Values may be sent and summed in bfloat16 or wider, within the bound.
A program may use at most 192 MiB of HBM per device.

```python
import math
import jax
import jax.numpy as jnp
from jax import lax

D = 384
HEADS = 6
HEAD_DIM = 64
FF = 1536
CLASSES = 1001
TSTEPS = 1000
SEQ = 256
LAT_DEV = 16
LATENTS = 512
PARAMS = 2659584
PARAMS_PAD = 2662400


def draw_params(key, part):
    pieces_spec = ((6 * D * D, 0.8 / D ** 0.5), (6 * D, 0.5), (3 * D * D, 1.0 / D ** 0.5), (D, 0.5), (D, 0.5), (D * D, 3.0 / D ** 0.5), (D, 0.3), (D * FF, 1.0 / D ** 0.5), (FF, 0.5), (FF * D, 1.0 / FF ** 0.5), (D, 0.3), (PARAMS_PAD - PARAMS, 0.5))
    drawn = []
    for number, (amount, spread) in enumerate(pieces_spec):
        normal = jax.random.normal(jax.random.fold_in(key, number), (amount,), jnp.float32)
        drawn.append(jnp.clip(normal, -3.0, 3.0) * spread)
    return jnp.concatenate(drawn).astype(jnp.bfloat16)


def with_ends(entries, rng, least, high):
    shape = entries.shape
    spot = [jax.random.randint(jax.random.fold_in(rng, axis), (), 0, shape[axis]) for axis in range(len(shape))]
    entries = entries.at[tuple(spot)].set(least)
    longest = shape.index(max(shape))
    spot[longest] = (spot[longest] + 1) % shape[longest]
    return entries.at[tuple(spot)].set(high)


def block_levels(own_key, dims, shards, least, top_value):
    level, own = 1.0, jax.random.fold_in(own_key, 6)
    for position, parts in shards:
        steps = jnp.exp(jax.random.uniform(jax.random.fold_in(own, position), (parts,), jnp.float32, least / len(shards), top_value / len(shards)))
        level = level * jnp.repeat(steps, dims[position] // parts).reshape([-1 if axis == position else 1 for axis in range(len(dims))])
    return level


def bell_draw(key, shape, width, reach, cuts=(), held_as=jnp.bfloat16):
    factor_of = block_levels(key, shape, cuts, -0.22, 0.18) if cuts else 1.0
    array = jax.random.normal(key, shape, jnp.float32) * width * factor_of
    return jnp.minimum(jnp.maximum(array, -reach), reach).astype(held_as)


def setup_inputs(seed: int = 0) -> dict:
    key_of = jax.random.split(jax.random.key(seed), 8)
    return {
        "latents_in": bell_draw(key_of[0], (LATENTS, SEQ, D), 1.0, 6.0, ((0, 32),)),
        "class_ids": with_ends(jax.random.randint(key_of[1], (LATENTS,), 0, CLASSES), jax.random.fold_in(key_of[1], 1), 0, CLASSES - 1).astype(jnp.int32),
        "step_ids": with_ends(jax.random.randint(key_of[2], (LATENTS,), 0, TSTEPS), jax.random.fold_in(key_of[2], 1), 0, TSTEPS - 1).astype(jnp.int32),
        "class_table": bell_draw(key_of[3], (CLASSES, D), 0.7, 4.1875),
        "step_table": bell_draw(key_of[4], (TSTEPS, D), 0.7, 4.1875),
        "params": draw_params(jax.random.fold_in(key_of[7], 71), 0),
        "cotangent": bell_draw(key_of[6], (LATENTS, SEQ, D), 1.0, 6.0, ((0, 32),)),
    }


@jax.custom_vjp
def low(v):
    return lax.optimization_barrier(v.astype(jnp.bfloat16)).astype(jnp.float32)

@jax.custom_vjp
def low_back(v):
    return v

def low_keep(v):
    return (low(v), None)

def low_pass(kept, grad):
    return (grad,)

def back_keep(v):
    return (v, None)

def back_low(kept, grad):
    return (low(grad),)
low.defvjp(low_keep, low_pass)
low_back.defvjp(back_keep, back_low)

def carve(flat_params):
    shapes = ((D, 6 * D), (6 * D,), (D, 3 * D), (D,), (D,), (D, D), (D,), (D, FF), (FF,), (FF, D), (D,))
    pieces = []
    offset = 0
    for extent in shapes:
        number = math.prod(extent)
        pieces.append(flat_params[offset:offset + number].reshape(extent))
        offset = offset + number
    return pieces

def normalize(values):
    average = lax.optimization_barrier(jnp.mean(values, axis=-1, keepdims=True))
    centered = values - average
    return centered * lax.rsqrt(lax.optimization_barrier(jnp.mean(centered * centered, axis=-1, keepdims=True)) + 1e-06)

def forward(flat_params, latents, condition):
    highest = lax.Precision.HIGHEST
    ada_w, ada_b, qkv_w, q_b, v_b, out_w, out_b, fc1_w, fc1_b, fc2_w, fc2_b = carve(flat_params)
    batch_count = latents.shape[0]
    modulation = low_back(jnp.dot(low(jax.nn.silu(condition)), ada_w, precision=highest) + ada_b)
    shift_a, scale_a, gate_a, shift_m, scale_m, gate_m = [modulation[:, None, column * D:(column + 1) * D] for column in range(6)]
    hidden_a = low((normalize(latents) * (1.0 + scale_a) + shift_a).reshape(-1, D))
    qkv_bias = jnp.concatenate([q_b, jnp.zeros_like(q_b), v_b])
    projected = low_back(low(jnp.dot(hidden_a, qkv_w, precision=highest) + qkv_bias))
    heads_view = projected.reshape(batch_count, SEQ, 3, HEADS, HEAD_DIM)
    scores = low_back(jnp.einsum('lshd,lthd->lhst', heads_view[:, :, 0], heads_view[:, :, 1], precision=highest) * HEAD_DIM ** (-0.5))
    probs = low(jax.nn.softmax(scores, axis=-1))
    context = low_back(low(jnp.einsum('lhst,lthd->lshd', probs, heads_view[:, :, 2], precision=highest).reshape(-1, D)))
    attended = low_back(jnp.dot(context, out_w, precision=highest) + out_b).reshape(batch_count, SEQ, D)
    resid_a = latents + gate_a * attended
    hidden_m = low((normalize(resid_a) * (1.0 + scale_m) + shift_m).reshape(-1, D))
    pre_act = low_back(jnp.dot(hidden_m, fc1_w, precision=highest) + fc1_b)
    activated = low(jax.nn.gelu(pre_act, approximate=True))
    mlp_out = low_back(jnp.dot(activated, fc2_w, precision=highest) + fc2_b).reshape(batch_count, SEQ, D)
    return resid_a + gate_m * mlp_out

def reference(latents_in, class_ids, step_ids, class_table, step_table, params, cotangent):
    flat_params = params.astype(jnp.float32)
    condition = class_table[class_ids].astype(jnp.float32) + step_table[step_ids].astype(jnp.float32)
    batch_groups = LATENTS // LAT_DEV

    def group_step(running, pieces):
        latent_block, cond_block, cot_block = pieces
        outputs, pullback = jax.vjp(forward, flat_params, latent_block.astype(jnp.float32), cond_block)
        grad_flat, grad_latent, grad_cond = pullback(cot_block.astype(jnp.float32))
        return (running + grad_flat, (outputs.astype(jnp.bfloat16), grad_latent.astype(jnp.bfloat16), grad_cond))
    inputs = (latents_in.reshape(batch_groups, LAT_DEV, SEQ, D), condition.reshape(batch_groups, LAT_DEV, D), cotangent.reshape(batch_groups, LAT_DEV, SEQ, D))
    running, (outputs, grad_latents, grad_conds) = lax.scan(group_step, jnp.zeros((PARAMS_PAD,), jnp.float32), inputs)
    return (outputs.reshape(LATENTS, SEQ, D), grad_latents.reshape(LATENTS, SEQ, D), grad_conds.reshape(LATENTS, D), running)
```

```python
from functools import partial
import math

import jax
import jax.numpy as jnp
from jax import lax
from jax.experimental import pallas as pl
from jax.experimental.pallas import tpu as pltpu
from jax.sharding import PartitionSpec as P

D = 384
HEADS = 6
HEAD_DIM = 64
FF = 1536
SEQ = 256
LANE = 128
CHUNK = 512
F32 = jnp.float32
BF16 = jnp.bfloat16
LOG2E = math.log2(math.e)
GELU_C = math.sqrt(2.0 / math.pi)

SHAPES = (
    ("ada_w", D, 6 * D),
    ("ada_b", 1, 6 * D),
    ("qkv_w", D, 3 * D),
    ("q_b", 1, D),
    ("v_b", 1, D),
    ("out_w", D, D),
    ("out_b", 1, D),
    ("fc1_w", D, FF),
    ("fc1_b", 1, FF),
    ("fc2_w", FF, D),
    ("fc2_b", 1, D),
)
PLACE = {}
USED = 0
for _name, _rows, _cols in SHAPES:
    PLACE[_name] = (USED, _rows, _cols // LANE)
    USED += _rows * _cols // LANE


def dot(a, b):
    return jnp.dot(a, b, preferred_element_type=F32)


def dot_nt(a, b):
    return lax.dot_general(a, b, (((1,), (1,)), ((), ())), preferred_element_type=F32)


def dot_tn(a, b):
    return lax.dot_general(a, b, (((0,), (0,)), ((), ())), preferred_element_type=F32)


def load_piece(flat, name, column):
    start, rows, width = PLACE[name]
    if rows == 1:
        return flat[start + column : start + column + 1, :]
    return flat[pl.ds(start + column, rows, stride=width), :]


def store_piece(flat, name, column, value):
    start, rows, width = PLACE[name]
    if rows == 1:
        flat[start + column : start + column + 1, :] = value
    else:
        flat[pl.ds(start + column, rows, stride=width), :] = value


def layer_norm(values):
    average = jnp.mean(values, axis=-1, keepdims=True)
    centered = values - average
    inv_std = lax.rsqrt(jnp.mean(centered * centered, axis=-1, keepdims=True) + 1e-06)
    return centered * inv_std, inv_std


def norm_back(grad, normed, inv_std):
    mean_grad = jnp.mean(grad, axis=-1, keepdims=True)
    mean_proj = jnp.mean(grad * normed, axis=-1, keepdims=True)
    return inv_std * (grad - mean_grad - normed * mean_proj)


def column_sum(values):
    return jnp.sum(values, axis=0, keepdims=True)


def block_kernel(
    steps,
    lat_ref,
    cot_ref,
    cond_ref,
    par_ref,
    out_ref,
    glat_ref,
    gcond_ref,
    flat_ref,
    ada_w,
    qkv_w,
    out_w,
    fc1_w,
    fc2_w,
    qkv_t,
    out_t,
    fc1_t,
    fc2_t,
    biases,
    mod_ref,
    gmod_ref,
    d_qkv,
    d_out,
    d_fc1,
    d_fc2t,
    d_qkvb,
    d_outb,
    d_fc1b,
    d_fc2b,
):
    step = pl.program_id(0)
    tall = par_ref.shape[0]

    @pl.when(step == 0)
    def _():
        flat_ref[...] = par_ref[...].astype(F32)
        for name, ref in (
            ("ada_w", ada_w),
            ("qkv_w", qkv_w),
            ("out_w", out_w),
            ("fc1_w", fc1_w),
            ("fc2_w", fc2_w),
        ):
            for column in range(PLACE[name][2]):
                ref[:, column * LANE : (column + 1) * LANE] = load_piece(
                    flat_ref, name, column
                ).astype(BF16)
        qkv_t[...] = qkv_w[...].T
        out_t[...] = out_w[...].T
        fc1_t[...] = fc1_w[...].T
        fc2_t[...] = fc2_w[...].T
        biases[...] = jnp.zeros_like(biases)
        for row, (name, first) in enumerate(
            (("ada_b", 0), ("q_b", 0), ("v_b", 2 * D), ("out_b", 0), ("fc1_b", 0), ("fc2_b", 0))
        ):
            row = (0, 1, 1, 2, 3, 4)[row]
            for column in range(PLACE[name][2]):
                left = first + column * LANE
                biases[row : row + 1, left : left + LANE] = load_piece(flat_ref, name, column)
        cond = cond_ref[...]
        silu = (cond * jax.nn.sigmoid(cond)).astype(BF16)
        mod_ref[...] = dot(silu, ada_w[...]) + biases[0:1, :]
        for ref in (d_qkv, d_out, d_fc1, d_fc2t, d_qkvb, d_outb, d_fc1b, d_fc2b):
            ref[...] = jnp.zeros_like(ref)

    mod = mod_ref[pl.ds(step, 1), :]
    shift_a, scale_a, gate_a, shift_m, scale_m, gate_m = [
        mod[:, n * D : (n + 1) * D] for n in range(6)
    ]
    x = lat_ref[0].astype(F32)
    cot = cot_ref[0].astype(F32)
    normed_a, inv_a = layer_norm(x)
    hidden_a = (normed_a * (1.0 + scale_a) + shift_a).astype(BF16)
    qkv = (dot(hidden_a, qkv_w[...]) + biases[1:2, : 3 * D]).astype(BF16)
    query = qkv[:, :D] * BF16(HEAD_DIM**-0.5)
    key = qkv[:, D : 2 * D]
    value = qkv[:, 2 * D :]
    key_t = key.T * BF16(HEAD_DIM**-0.5)
    value_t = value.T
    low_half = lax.broadcasted_iota(jnp.int32, (SEQ, LANE), 1) < HEAD_DIM
    zero = jnp.zeros((SEQ, LANE), BF16)

    def half(values, head):
        return jnp.where(low_half, values, zero) if head % 2 == 0 else jnp.where(low_half, zero, values)

    def pair(values, head):
        left = head // 2 * LANE
        return values[:, left : left + LANE]

    probs = []
    probs_b = []
    ctx_rows = []
    for head in range(HEADS):
        rows = slice(head * HEAD_DIM, (head + 1) * HEAD_DIM)
        scores = dot_nt(half(pair(key, head), head), pair(query, head)) * LOG2E
        grown = jnp.exp2(scores - jnp.max(scores, axis=0, keepdims=True))
        prob = grown * (1.0 / column_sum(grown))
        prob_b = prob.astype(BF16)
        probs.append(prob)
        probs_b.append(prob_b)
        ctx_rows.append(dot(value_t[rows, :], prob_b).astype(BF16))
    ctx_t = jnp.concatenate(ctx_rows, axis=0)
    attended = dot(ctx_t.T, out_w[...]) + biases[2:3, :D]
    resid = x + gate_a * attended
    normed_m, inv_m = layer_norm(resid)
    hidden_m = (normed_m * (1.0 + scale_m) + shift_m).astype(BF16)
    hidden_mt = hidden_m.T
    g_mlp = (cot * gate_m).astype(BF16)
    g_mlpt = g_mlp.T
    d_fc2b[...] += column_sum(g_mlp.astype(F32))
    mlp_out = biases[4:5, :D]
    g_hidden_m = None
    for left in range(0, FF, CHUNK):
        cols = slice(left, left + CHUNK)
        pre = dot(hidden_m, fc1_w[:, cols]) + biases[3:4, cols]
        square = pre * pre
        gate = 0.5 + 0.5 * jnp.tanh(pre * (GELU_C + (GELU_C * 0.044715) * square))
        act = pre * gate
        slope = gate + act * (1.0 - gate) * (2.0 * GELU_C + (6.0 * GELU_C * 0.044715) * square)
        act_b = act.astype(BF16)
        mlp_out = mlp_out + dot(act_b, fc2_w[cols, :])
        g_pre = dot(g_mlp, fc2_t[:, cols]) * slope
        g_pre_b = g_pre.astype(BF16)
        part = dot(g_pre_b, fc1_t[cols, :])
        g_hidden_m = part if g_hidden_m is None else g_hidden_m + part
        d_fc2t[:, cols] += dot(g_mlpt, act_b)
        d_fc1[:, cols] += dot(hidden_mt, g_pre_b)
        d_fc1b[:, cols] += column_sum(g_pre_b.astype(F32))
    out_ref[0] = (resid + gate_m * mlp_out).astype(BF16)
    g_gate_m = column_sum(cot * mlp_out)
    g_shift_m = column_sum(g_hidden_m)
    g_scale_m = column_sum(g_hidden_m * normed_m)
    g_resid = cot + norm_back(g_hidden_m * (1.0 + scale_m), normed_m, inv_m)
    g_gate_a = column_sum(g_resid * attended)
    g_attn = (g_resid * gate_a).astype(BF16)
    d_out[...] += dot(ctx_t, g_attn)
    d_outb[...] += column_sum(g_attn.astype(F32))
    g_ctx = dot(g_attn, out_t[...]).astype(BF16)
    gq_rows = []
    g_keys = []
    g_values = []
    for head in range(HEADS):
        rows = slice(head * HEAD_DIM, (head + 1) * HEAD_DIM)
        g_prob = dot_nt(half(pair(value, head), head), pair(g_ctx, head))
        prob = probs[head]
        g_score = (prob * (g_prob - column_sum(g_prob * prob))).astype(BF16)
        gq_rows.append(dot(key_t[rows, :], g_score).astype(BF16))
        g_key = dot(g_score, pair(query, head))
        g_value = dot(probs_b[head], pair(g_ctx, head))
        if head % 2 == 0:
            even = (g_key, g_value)
        else:
            g_keys.append(jnp.where(low_half, even[0], g_key).astype(BF16))
            g_values.append(jnp.where(low_half, even[1], g_value).astype(BF16))
    g_query = jnp.concatenate(gq_rows, axis=0).T
    g_qkv = jnp.concatenate([g_query] + g_keys + g_values, axis=1)
    d_qkv[...] += dot(hidden_a.T, g_qkv)
    d_qkvb[...] += column_sum(g_qkv.astype(F32))
    g_hidden_a = dot(g_qkv, qkv_t[...])
    g_shift_a = column_sum(g_hidden_a)
    g_scale_a = column_sum(g_hidden_a * normed_a)
    glat_ref[0] = (
        g_resid + norm_back(g_hidden_a * (1.0 + scale_a), normed_a, inv_a)
    ).astype(BF16)
    gmod_ref[pl.ds(step, 1), :] = jnp.concatenate(
        [g_shift_a, g_scale_a, g_gate_a, g_shift_m, g_scale_m, g_gate_m], axis=1
    )

    @pl.when(step == steps - 1)
    def _():
        cond = cond_ref[...]
        sig = jax.nn.sigmoid(cond)
        silu = (cond * sig).astype(BF16)
        g_mod = gmod_ref[...].astype(BF16)
        gcond_ref[...] = dot_nt(g_mod, ada_w[...]) * (sig * (1.0 + cond * (1.0 - sig)))
        mod_sum = column_sum(g_mod.astype(F32))

        def put(name, value, first=0):
            for column in range(PLACE[name][2]):
                left = first + column * LANE
                store_piece(flat_ref, name, column, value[:, left : left + LANE])

        for column in range(0, 6 * D, D):
            part = dot_tn(silu, g_mod[:, column : column + D])
            for inner in range(D // LANE):
                store_piece(
                    flat_ref,
                    "ada_w",
                    column // LANE + inner,
                    part[:, inner * LANE : (inner + 1) * LANE],
                )
        put("ada_b", mod_sum)
        put("qkv_w", d_qkv)
        put("q_b", d_qkvb)
        put("v_b", d_qkvb, 2 * D)
        put("out_w", d_out)
        put("out_b", d_outb)
        put("fc1_w", d_fc1)
        put("fc1_b", d_fc1b)
        for column in range(D // LANE):
            store_piece(
                flat_ref, "fc2_w", column, d_fc2t[column * LANE : (column + 1) * LANE, :].T
            )
        put("fc2_b", d_fc2b)
        flat_ref[USED:tall, :] = jnp.zeros((tall - USED, LANE), F32)


def run_block(latents, cotangent, condition, flat):
    count = latents.shape[0]
    tall = flat.shape[0]
    once = pl.Buffered(1)
    latent_spec = pl.BlockSpec((1, SEQ, D), lambda i: (i, 0, 0))
    return pl.pallas_call(
        partial(block_kernel, count),
        grid=(count,),
        in_specs=[
            latent_spec,
            latent_spec,
            pl.BlockSpec((count, D), lambda i: (0, 0), pipeline_mode=once),
            pl.BlockSpec((tall, LANE), lambda i: (0, 0), pipeline_mode=once),
        ],
        out_specs=[
            latent_spec,
            latent_spec,
            pl.BlockSpec((count, D), lambda i: (0, 0), pipeline_mode=once),
            pl.BlockSpec((tall, LANE), lambda i: (0, 0), pipeline_mode=once),
        ],
        out_shape=[
            jax.ShapeDtypeStruct(latents.shape, BF16),
            jax.ShapeDtypeStruct(latents.shape, BF16),
            jax.ShapeDtypeStruct((count, D), F32),
            jax.ShapeDtypeStruct((tall, LANE), F32),
        ],
        scratch_shapes=[
            pltpu.VMEM((D, 6 * D), BF16),
            pltpu.VMEM((D, 3 * D), BF16),
            pltpu.VMEM((D, D), BF16),
            pltpu.VMEM((D, FF), BF16),
            pltpu.VMEM((FF, D), BF16),
            pltpu.VMEM((3 * D, D), BF16),
            pltpu.VMEM((D, D), BF16),
            pltpu.VMEM((FF, D), BF16),
            pltpu.VMEM((D, FF), BF16),
            pltpu.VMEM((8, 6 * D), F32),
            pltpu.VMEM((count, 6 * D), F32),
            pltpu.VMEM((count, 6 * D), F32),
            pltpu.VMEM((D, 3 * D), F32),
            pltpu.VMEM((D, D), F32),
            pltpu.VMEM((D, FF), F32),
            pltpu.VMEM((D, FF), F32),
            pltpu.VMEM((1, 3 * D), F32),
            pltpu.VMEM((1, D), F32),
            pltpu.VMEM((1, FF), F32),
            pltpu.VMEM((1, D), F32),
        ],
        compiler_params=pltpu.CompilerParams(
            dimension_semantics=("arbitrary",), vmem_limit_bytes=60 * 1024 * 1024
        ),
    )(latents, cotangent, condition, flat)


def on_device(latents_in, class_ids, step_ids, class_table, step_table, params, cotangent):
    flat = lax.all_gather(params.reshape(-1, LANE), "dp", axis=0, tiled=True)
    class_hot = (
        class_ids[:, None] == jnp.arange(class_table.shape[0], dtype=jnp.int32)[None, :]
    ).astype(BF16)
    step_hot = (
        step_ids[:, None] == jnp.arange(step_table.shape[0], dtype=jnp.int32)[None, :]
    ).astype(BF16)
    condition = dot(class_hot, class_table) + dot(step_hot, step_table)
    block_out, grad_latents, grad_condition, grad_flat = run_block(
        latents_in, cotangent, condition, flat
    )
    grad_params = lax.psum_scatter(grad_flat, "dp", scatter_dimension=0, tiled=True)
    return block_out, grad_latents, grad_condition, grad_params.reshape(-1)


def solution(mesh):
    in_specs = (P("dp", None, None), P("dp"), P("dp"), P(), P(), P("dp"), P("dp", None, None))
    out_specs = (P("dp", None, None), P("dp", None, None), P("dp", None), P("dp"))
    return jax.shard_map(
        on_device, mesh=mesh, in_specs=in_specs, out_specs=out_specs, check_vma=False
    )
```

```python
from functools import partial
import math

import jax
import jax.numpy as jnp
from jax import lax
from jax.experimental import pallas as pl
from jax.experimental.pallas import tpu as pltpu
from jax.sharding import PartitionSpec as P

D = 384
HEADS = 6
HEAD_DIM = 64
FF = 1536
SEQ = 256
LANE = 128
CHUNK = 512
PER = 2
F32 = jnp.float32
BF16 = jnp.bfloat16
LOG2E = math.log2(math.e)
GELU_C = math.sqrt(2.0 / math.pi)

SHAPES = (
    ("ada_w", D, 6 * D),
    ("ada_b", 1, 6 * D),
    ("qkv_w", D, 3 * D),
    ("q_b", 1, D),
    ("v_b", 1, D),
    ("out_w", D, D),
    ("out_b", 1, D),
    ("fc1_w", D, FF),
    ("fc1_b", 1, FF),
    ("fc2_w", FF, D),
    ("fc2_b", 1, D),
)
PLACE = {}
USED = 0
for _name, _rows, _cols in SHAPES:
    PLACE[_name] = (USED, _rows, _cols // LANE)
    USED += _rows * _cols // LANE


def bit_orders(count):
    bits = list(range(count.bit_length() - 1))
    return bits, bits[:1] + bits[2:3] + bits[1:2] + bits[3:]


def place_of(owner, order):
    place = 0
    for bit in order:
        place = place * 2 + owner // 2**bit % 2
    return place


def partner_of(me, bit):
    return me + (1 - 2 * (me // 2**bit % 2)) * 2**bit


def greet(me, bits):
    barrier = pltpu.get_barrier_semaphore()
    for bit in range(bits):
        pl.semaphore_signal(
            barrier,
            inc=1,
            device_id=(partner_of(me, bit),),
            device_id_type=pl.DeviceIdType.MESH,
        )
    pl.semaphore_wait(barrier, bits)


def gather_kernel(count, mine_ref, all_ref, own_sem, send_sem, recv_sem, hand_send, hand_recv):
    me = lax.axis_index("dp")
    orders = bit_orders(count)
    bits = len(orders[0])
    places = [place_of(me, order) for order in orders]
    own = [
        pltpu.make_async_copy(mine_ref.at[lane], all_ref.at[lane, places[lane]], own_sem.at[lane])
        for lane in range(2)
    ]
    for copy in own:
        copy.start()
    greet(me, bits)

    def start(lane, stage):
        size = 2**stage
        held = all_ref.at[lane, pl.ds(places[lane] // size * size, size)]
        copy = pltpu.make_async_remote_copy(
            src_ref=held,
            dst_ref=held,
            send_sem=send_sem.at[lane, stage],
            recv_sem=recv_sem.at[lane, stage],
            device_id=(partner_of(me, orders[lane][bits - 1 - stage]),),
            device_id_type=pl.DeviceIdType.MESH,
        )
        copy.start()
        return copy

    def hand_over(lane, stage):
        size = 1 if stage == 0 else 2 ** (stage - 1)
        first = places[lane] // size
        if stage > 0:
            first = first + 1 - 2 * (first % 2)
        held = all_ref.at[lane, pl.ds(first * size, size)]
        copy = pltpu.make_async_remote_copy(
            src_ref=held,
            dst_ref=held,
            send_sem=hand_send.at[lane, stage],
            recv_sem=hand_recv.at[lane, stage],
            device_id=(partner_of(me, 0),),
            device_id_type=pl.DeviceIdType.MESH,
        )
        copy.start()
        return copy

    flying = []
    handed = []
    for lane in range(2):
        own[lane].wait()
        flying.append(start(lane, 0))
        handed.append(hand_over(lane, 0))
    for stage in range(1, bits):
        for lane in range(2):
            flying[lane].wait()
            if stage < bits - 1:
                flying[lane] = start(lane, stage)
            handed.append(hand_over(lane, stage))
    for copy in handed:
        copy.wait()


def gather(mine, count):
    lanes, half, width = mine.shape
    bits = count.bit_length() - 1
    return pl.pallas_call(
        partial(gather_kernel, count),
        in_specs=[pl.BlockSpec(memory_space=pltpu.VMEM)],
        out_specs=pl.BlockSpec(memory_space=pltpu.VMEM),
        out_shape=jax.ShapeDtypeStruct((lanes, count, half, width), mine.dtype),
        scratch_shapes=[
            pltpu.SemaphoreType.DMA((2,)),
            pltpu.SemaphoreType.DMA((2, bits)),
            pltpu.SemaphoreType.DMA((2, bits)),
            pltpu.SemaphoreType.DMA((2, bits)),
            pltpu.SemaphoreType.DMA((2, bits)),
        ],
        compiler_params=pltpu.CompilerParams(
            collective_id=0, has_side_effects=True, vmem_limit_bytes=40 * 1024 * 1024
        ),
    )(mine)


def reduce_kernel(count, all_ref, sum_ref, land_ref, send_sem, recv_sem):
    me = lax.axis_index("dp")
    orders = bit_orders(count)
    bits = len(orders[0])
    places = [place_of(me, order) for order in orders]
    greet(me, bits)

    def start(lane, stage):
        size = count // 2 ** (stage + 1)
        side = places[lane] // size % 2
        if stage == 0:
            source = all_ref.at[lane, pl.ds((1 - side) * size, size)]
        else:
            source = land_ref.at[lane, pl.ds(2 * size + (1 - side) * size, size)]
        copy = pltpu.make_async_remote_copy(
            src_ref=source,
            dst_ref=land_ref.at[lane, pl.ds(size, size)],
            send_sem=send_sem.at[lane, stage],
            recv_sem=recv_sem.at[lane, stage],
            device_id=(partner_of(me, orders[lane][stage]),),
            device_id_type=pl.DeviceIdType.MESH,
        )
        copy.start()
        return copy

    def add(lane, stage):
        size = count // 2 ** (stage + 1)
        side = places[lane] // size % 2

        def one(block):
            if stage == 0:
                kept = all_ref[lane, side * size + block]
            else:
                kept = land_ref[lane, 2 * size + side * size + block]
            return kept.astype(F32) + land_ref[lane, size + block].astype(F32)

        if stage == bits - 1:
            sum_ref[lane] = one(0)
        else:

            def body(block, carry):
                land_ref[lane, size + block] = one(block).astype(BF16)
                return carry

            lax.fori_loop(0, size, body, 0)

    flying = [start(lane, 0) for lane in range(2)]
    for stage in range(bits):
        for lane in range(2):
            flying[lane].wait()
            add(lane, stage)
            if stage < bits - 1:
                flying[lane] = start(lane, stage + 1)


def reduce(parts):
    lanes, count, half, width = parts.shape
    bits = count.bit_length() - 1
    return pl.pallas_call(
        partial(reduce_kernel, count),
        in_specs=[pl.BlockSpec(memory_space=pltpu.VMEM)],
        out_specs=pl.BlockSpec(memory_space=pltpu.VMEM),
        out_shape=jax.ShapeDtypeStruct((lanes, half, width), F32),
        scratch_shapes=[
            pltpu.VMEM((lanes, count, half, width), BF16),
            pltpu.SemaphoreType.DMA((2, bits)),
            pltpu.SemaphoreType.DMA((2, bits)),
        ],
        compiler_params=pltpu.CompilerParams(
            collective_id=1, has_side_effects=True, vmem_limit_bytes=40 * 1024 * 1024
        ),
    )(parts)


def dot(a, b):
    return jnp.dot(a, b, preferred_element_type=F32)


def dot_nt(a, b):
    return lax.dot_general(a, b, (((1,), (1,)), ((), ())), preferred_element_type=F32)


def dot_tn(a, b):
    return lax.dot_general(a, b, (((0,), (0,)), ((), ())), preferred_element_type=F32)


def load_piece(flat, name, column):
    start, rows, width = PLACE[name]
    if rows == 1:
        return flat[start + column : start + column + 1, :]
    return flat[pl.ds(start + column, rows, stride=width), :]


def store_piece(flat, name, column, value):
    start, rows, width = PLACE[name]
    if rows == 1:
        flat[start + column : start + column + 1, :] = value
    else:
        flat[pl.ds(start + column, rows, stride=width), :] = value


def layer_norm(values):
    average = jnp.mean(values, axis=-1, keepdims=True)
    centered = values - average
    inv_std = lax.rsqrt(jnp.mean(centered * centered, axis=-1, keepdims=True) + 1e-06)
    return centered * inv_std, inv_std


def norm_back(grad, normed, inv_std):
    mean_grad = jnp.mean(grad, axis=-1, keepdims=True)
    mean_proj = jnp.mean(grad * normed, axis=-1, keepdims=True)
    return inv_std * (grad - mean_grad - normed * mean_proj)


def column_sum(values):
    return jnp.sum(values, axis=0, keepdims=True)


def block_kernel(
    steps,
    rows,
    lat_ref,
    cot_ref,
    cond_ref,
    par_ref,
    out_ref,
    glat_ref,
    gcond_ref,
    gpar_ref,
    flat_ref,
    ada_w,
    qkv_w,
    out_w,
    fc1_w,
    fc2_w,
    qkv_t,
    out_t,
    fc1_t,
    fc2_t,
    biases,
    mod_ref,
    gmod_ref,
    d_qkv,
    d_out,
    d_fc1,
    d_fc2t,
    d_qkvb,
    d_outb,
    d_fc1b,
    d_fc2b,
):
    step = pl.program_id(0)
    owners, half_rows = par_ref.shape[1:3]
    tall = owners * rows
    orders = bit_orders(owners)
    spans = ((0, half_rows), (half_rows, rows))

    @pl.when(step == 0)
    def _():
        for owner in range(owners):
            for lane, (first, last) in enumerate(spans):
                flat_ref[owner * rows + first : owner * rows + last, :] = par_ref[
                    lane, place_of(owner, orders[lane])
                ].astype(F32)[: last - first]
        for name, ref in (
            ("ada_w", ada_w),
            ("qkv_w", qkv_w),
            ("out_w", out_w),
            ("fc1_w", fc1_w),
            ("fc2_w", fc2_w),
        ):
            for column in range(PLACE[name][2]):
                ref[:, column * LANE : (column + 1) * LANE] = load_piece(
                    flat_ref, name, column
                ).astype(BF16)
        qkv_t[...] = qkv_w[...].T
        out_t[...] = out_w[...].T
        fc1_t[...] = fc1_w[...].T
        fc2_t[...] = fc2_w[...].T
        biases[...] = jnp.zeros_like(biases)
        for row, (name, first) in enumerate(
            (("ada_b", 0), ("q_b", 0), ("v_b", 2 * D), ("out_b", 0), ("fc1_b", 0), ("fc2_b", 0))
        ):
            row = (0, 1, 1, 2, 3, 4)[row]
            for column in range(PLACE[name][2]):
                left = first + column * LANE
                biases[row : row + 1, left : left + LANE] = load_piece(flat_ref, name, column)
        cond = cond_ref[...]
        silu = (cond * jax.nn.sigmoid(cond)).astype(BF16)
        mod_ref[...] = dot(silu, ada_w[...]) + biases[0:1, :]
        for ref in (d_qkv, d_out, d_fc1, d_fc2t, d_qkvb, d_outb, d_fc1b, d_fc2b):
            ref[...] = jnp.zeros_like(ref)

    each = range(PER)
    mods = [mod_ref[pl.ds(step * PER + n, 1), :] for n in each]
    shift_a, scale_a, gate_a, shift_m, scale_m, gate_m = [
        [mods[n][:, piece * D : (piece + 1) * D] for n in each] for piece in range(6)
    ]

    def join(parts):
        return jnp.concatenate(parts, axis=0)

    def cut(values):
        return [values[n * SEQ : (n + 1) * SEQ] for n in each]

    low_half = lax.broadcasted_iota(jnp.int32, (SEQ, LANE), 1) < HEAD_DIM
    zero = jnp.zeros((SEQ, LANE), BF16)

    def half(values, head):
        return jnp.where(low_half, values, zero) if head % 2 == 0 else jnp.where(low_half, zero, values)

    def pair(values, head):
        left = head // 2 * LANE
        return values[:, left : left + LANE]

    x = [lat_ref[n].astype(F32) for n in each]
    cot = [cot_ref[n].astype(F32) for n in each]
    normed_a, inv_a = zip(*[layer_norm(x[n]) for n in each])
    hidden_a = join(
        [(normed_a[n] * (1.0 + scale_a[n]) + shift_a[n]).astype(BF16) for n in each]
    )
    qkv = (dot(hidden_a, qkv_w[...]) + biases[1:2, : 3 * D]).astype(BF16)
    query = cut(qkv[:, :D] * BF16(HEAD_DIM**-0.5))
    key = cut(qkv[:, D : 2 * D])
    value = cut(qkv[:, 2 * D :])
    key_t = [key[n].T * BF16(HEAD_DIM**-0.5) for n in each]
    value_t = [value[n].T for n in each]
    probs = [[] for n in each]
    probs_b = [[] for n in each]
    ctx_rows = [[] for n in each]
    for head in range(HEADS):
        head_rows = slice(head * HEAD_DIM, (head + 1) * HEAD_DIM)
        for n in each:
            scores = dot_nt(half(pair(key[n], head), head), pair(query[n], head)) * LOG2E
            grown = jnp.exp2(scores - jnp.max(scores, axis=0, keepdims=True))
            prob = grown * (1.0 / column_sum(grown))
            prob_b = prob.astype(BF16)
            probs[n].append(prob)
            probs_b[n].append(prob_b)
            ctx_rows[n].append(dot(value_t[n][head_rows, :], prob_b).astype(BF16))
    ctx_t = jnp.concatenate([join(ctx_rows[n]) for n in each], axis=1)
    attended = cut(dot(ctx_t.T, out_w[...]) + biases[2:3, :D])
    resid = [x[n] + gate_a[n] * attended[n] for n in each]
    normed_m, inv_m = zip(*[layer_norm(resid[n]) for n in each])
    hidden_m = join(
        [(normed_m[n] * (1.0 + scale_m[n]) + shift_m[n]).astype(BF16) for n in each]
    )
    hidden_mt = hidden_m.T
    g_mlp = join([(cot[n] * gate_m[n]).astype(BF16) for n in each])
    g_mlpt = g_mlp.T
    d_fc2b[...] += column_sum(g_mlp.astype(F32))
    mlp_out = biases[4:5, :D]
    g_hidden_m = None
    for left in range(0, FF, CHUNK):
        cols = slice(left, left + CHUNK)
        pre = dot(hidden_m, fc1_w[:, cols]) + biases[3:4, cols]
        square = pre * pre
        gate = 0.5 + 0.5 * jnp.tanh(pre * (GELU_C + (GELU_C * 0.044715) * square))
        act = pre * gate
        slope = gate + act * (1.0 - gate) * (2.0 * GELU_C + (6.0 * GELU_C * 0.044715) * square)
        act_b = act.astype(BF16)
        mlp_out = mlp_out + dot(act_b, fc2_w[cols, :])
        g_pre = dot(g_mlp, fc2_t[:, cols]) * slope
        g_pre_b = g_pre.astype(BF16)
        part = dot(g_pre_b, fc1_t[cols, :])
        g_hidden_m = part if g_hidden_m is None else g_hidden_m + part
        d_fc2t[:, cols] += dot(g_mlpt, act_b)
        d_fc1[:, cols] += dot(hidden_mt, g_pre_b)
        d_fc1b[:, cols] += column_sum(g_pre_b.astype(F32))
    mlp_out = cut(mlp_out)
    g_hidden_m = cut(g_hidden_m)
    g_resid = []
    for n in each:
        out_ref[n] = (resid[n] + gate_m[n] * mlp_out[n]).astype(BF16)
        g_resid.append(
            cot[n] + norm_back(g_hidden_m[n] * (1.0 + scale_m[n]), normed_m[n], inv_m[n])
        )
    late_mod = [
        [
            column_sum(g_resid[n] * attended[n]),
            column_sum(g_hidden_m[n]),
            column_sum(g_hidden_m[n] * normed_m[n]),
            column_sum(cot[n] * mlp_out[n]),
        ]
        for n in each
    ]
    g_attn = join([(g_resid[n] * gate_a[n]).astype(BF16) for n in each])
    d_out[...] += dot(ctx_t, g_attn)
    d_outb[...] += column_sum(g_attn.astype(F32))
    g_ctx = cut(dot(g_attn, out_t[...]).astype(BF16))
    gq_rows = [[] for n in each]
    g_keys = [[] for n in each]
    g_values = [[] for n in each]
    even = [None for n in each]
    for head in range(HEADS):
        head_rows = slice(head * HEAD_DIM, (head + 1) * HEAD_DIM)
        for n in each:
            g_prob = dot_nt(half(pair(value[n], head), head), pair(g_ctx[n], head))
            prob = probs[n][head]
            g_score = (prob * (g_prob - column_sum(g_prob * prob))).astype(BF16)
            gq_rows[n].append(dot(key_t[n][head_rows, :], g_score).astype(BF16))
            g_key = dot(g_score, pair(query[n], head))
            g_value = dot(probs_b[n][head], pair(g_ctx[n], head))
            if head % 2 == 0:
                even[n] = (g_key, g_value)
            else:
                g_keys[n].append(jnp.where(low_half, even[n][0], g_key).astype(BF16))
                g_values[n].append(jnp.where(low_half, even[n][1], g_value).astype(BF16))
    g_qkv = join(
        [
            jnp.concatenate([join(gq_rows[n]).T] + g_keys[n] + g_values[n], axis=1)
            for n in each
        ]
    )
    d_qkv[...] += dot(hidden_a.T, g_qkv)
    d_qkvb[...] += column_sum(g_qkv.astype(F32))
    g_hidden_a = cut(dot(g_qkv, qkv_t[...]))
    for n in each:
        glat_ref[n] = (
            g_resid[n] + norm_back(g_hidden_a[n] * (1.0 + scale_a[n]), normed_a[n], inv_a[n])
        ).astype(BF16)
        gmod_ref[pl.ds(step * PER + n, 1), :] = jnp.concatenate(
            [column_sum(g_hidden_a[n]), column_sum(g_hidden_a[n] * normed_a[n])] + late_mod[n],
            axis=1,
        )

    @pl.when(step == steps - 1)
    def _():
        cond = cond_ref[...]
        sig = jax.nn.sigmoid(cond)
        silu = (cond * sig).astype(BF16)
        g_mod = gmod_ref[...].astype(BF16)
        gcond_ref[...] = dot_nt(g_mod, ada_w[...]) * (sig * (1.0 + cond * (1.0 - sig)))
        mod_sum = column_sum(g_mod.astype(F32))

        def put(name, value, first=0):
            for column in range(PLACE[name][2]):
                left = first + column * LANE
                store_piece(flat_ref, name, column, value[:, left : left + LANE])

        for column in range(0, 6 * D, D):
            part = dot_tn(silu, g_mod[:, column : column + D])
            for inner in range(D // LANE):
                store_piece(
                    flat_ref,
                    "ada_w",
                    column // LANE + inner,
                    part[:, inner * LANE : (inner + 1) * LANE],
                )
        put("ada_b", mod_sum)
        put("qkv_w", d_qkv)
        put("q_b", d_qkvb)
        put("v_b", d_qkvb, 2 * D)
        put("out_w", d_out)
        put("out_b", d_outb)
        put("fc1_w", d_fc1)
        put("fc1_b", d_fc1b)
        for column in range(D // LANE):
            store_piece(
                flat_ref, "fc2_w", column, d_fc2t[column * LANE : (column + 1) * LANE, :].T
            )
        put("fc2_b", d_fc2b)
        flat_ref[USED:tall, :] = jnp.zeros((tall - USED, LANE), F32)
        for owner in range(owners):
            for lane, (first, last) in enumerate(spans):
                block = flat_ref[owner * rows + first : owner * rows + last, :]
                if last - first < half_rows:
                    rest = jnp.zeros((half_rows - (last - first), LANE), F32)
                    block = jnp.concatenate([block, rest], axis=0)
                gpar_ref[lane, place_of(owner, orders[lane])] = block.astype(BF16)


def run_block(latents, cotangent, condition, flat, rows):
    count = latents.shape[0]
    once = pl.Buffered(1)
    latent_spec = pl.BlockSpec((PER, SEQ, D), lambda i: (i, 0, 0))
    return pl.pallas_call(
        partial(block_kernel, count // PER, rows),
        grid=(count // PER,),
        in_specs=[
            latent_spec,
            latent_spec,
            pl.BlockSpec((count, D), lambda i: (0, 0), pipeline_mode=once),
            pl.BlockSpec(flat.shape, lambda i: (0, 0, 0, 0), pipeline_mode=once),
        ],
        out_specs=[
            latent_spec,
            latent_spec,
            pl.BlockSpec((count, D), lambda i: (0, 0), pipeline_mode=once),
            pl.BlockSpec(flat.shape, lambda i: (0, 0, 0, 0), pipeline_mode=once),
        ],
        out_shape=[
            jax.ShapeDtypeStruct(latents.shape, BF16),
            jax.ShapeDtypeStruct(latents.shape, BF16),
            jax.ShapeDtypeStruct((count, D), F32),
            jax.ShapeDtypeStruct(flat.shape, BF16),
        ],
        scratch_shapes=[
            pltpu.VMEM((flat.shape[1] * rows, LANE), F32),
            pltpu.VMEM((D, 6 * D), BF16),
            pltpu.VMEM((D, 3 * D), BF16),
            pltpu.VMEM((D, D), BF16),
            pltpu.VMEM((D, FF), BF16),
            pltpu.VMEM((FF, D), BF16),
            pltpu.VMEM((3 * D, D), BF16),
            pltpu.VMEM((D, D), BF16),
            pltpu.VMEM((FF, D), BF16),
            pltpu.VMEM((D, FF), BF16),
            pltpu.VMEM((8, 6 * D), F32),
            pltpu.VMEM((count, 6 * D), F32),
            pltpu.VMEM((count, 6 * D), F32),
            pltpu.VMEM((D, 3 * D), F32),
            pltpu.VMEM((D, D), F32),
            pltpu.VMEM((D, FF), F32),
            pltpu.VMEM((D, FF), F32),
            pltpu.VMEM((1, 3 * D), F32),
            pltpu.VMEM((1, D), F32),
            pltpu.VMEM((1, FF), F32),
            pltpu.VMEM((1, D), F32),
        ],
        compiler_params=pltpu.CompilerParams(
            dimension_semantics=("arbitrary",), vmem_limit_bytes=60 * 1024 * 1024
        ),
    )(latents, cotangent, condition, flat)


def on_device(latents_in, class_ids, step_ids, class_table, step_table, params, cotangent):
    devices = lax.axis_size("dp")
    rows = params.shape[0] // LANE
    half_rows = -(-rows // 32) * 16
    mine = jnp.pad(params.reshape(rows, LANE), ((0, 2 * half_rows - rows), (0, 0)))
    flat = gather(mine.reshape(2, half_rows, LANE), devices)
    class_hot = (
        class_ids[:, None] == jnp.arange(class_table.shape[0], dtype=jnp.int32)[None, :]
    ).astype(BF16)
    step_hot = (
        step_ids[:, None] == jnp.arange(step_table.shape[0], dtype=jnp.int32)[None, :]
    ).astype(BF16)
    condition = dot(class_hot, class_table) + dot(step_hot, step_table)
    block_out, grad_latents, grad_condition, grad_flat = run_block(
        latents_in, cotangent, condition, flat, rows
    )
    grad_params = reduce(grad_flat).reshape(2 * half_rows, LANE)[:rows]
    return block_out, grad_latents, grad_condition, grad_params.reshape(-1)


def solution(mesh):
    in_specs = (P("dp", None, None), P("dp"), P("dp"), P(), P(), P("dp"), P("dp", None, None))
    out_specs = (P("dp", None, None), P("dp", None, None), P("dp", None), P("dp"))
    return jax.shard_map(
        on_device, mesh=mesh, in_specs=in_specs, out_specs=out_specs, check_vma=False
    )
```

```python
from functools import partial
import math

import jax
import jax.numpy as jnp
from jax import lax
from jax.experimental import pallas as pl
from jax.experimental.pallas import tpu as pltpu
from jax.sharding import PartitionSpec as P

D = 384
HEADS = 6
HEAD_DIM = 64
FF = 1536
SEQ = 256
LANE = 128
CHUNK = 512
PER = 2
F32 = jnp.float32
BF16 = jnp.bfloat16
LOG2E = math.log2(math.e)
GELU_C = math.sqrt(2.0 / math.pi)

SHAPES = (
    ("ada_w", D, 6 * D),
    ("ada_b", 1, 6 * D),
    ("qkv_w", D, 3 * D),
    ("q_b", 1, D),
    ("v_b", 1, D),
    ("out_w", D, D),
    ("out_b", 1, D),
    ("fc1_w", D, FF),
    ("fc1_b", 1, FF),
    ("fc2_w", FF, D),
    ("fc2_b", 1, D),
)
PLACE = {}
USED = 0
for _name, _rows, _cols in SHAPES:
    PLACE[_name] = (USED, _rows, _cols // LANE)
    USED += _rows * _cols // LANE


def bit_orders(count):
    bits = list(range(count.bit_length() - 1))
    return bits, bits[:1] + bits[2:3] + bits[1:2] + bits[3:]


def place_of(owner, order):
    place = 0
    for bit in order:
        place = place * 2 + owner // 2**bit % 2
    return place


def partner_of(me, bit):
    return me + (1 - 2 * (me // 2**bit % 2)) * 2**bit


def greet(me, bits):
    barrier = pltpu.get_barrier_semaphore()
    for bit in range(bits):
        pl.semaphore_signal(
            barrier,
            inc=1,
            device_id=(partner_of(me, bit),),
            device_id_type=pl.DeviceIdType.MESH,
        )
    pl.semaphore_wait(barrier, bits)


def gather_kernel(count, mine_ref, all_ref, own_sem, send_sem, recv_sem, hand_send, hand_recv):
    me = lax.axis_index("dp")
    orders = bit_orders(count)
    bits = len(orders[0])
    places = [place_of(me, order) for order in orders]
    own = [
        pltpu.make_async_copy(mine_ref.at[lane], all_ref.at[lane, places[lane]], own_sem.at[lane])
        for lane in range(2)
    ]
    for copy in own:
        copy.start()
    greet(me, bits)

    def start(lane, stage):
        size = 2**stage
        held = all_ref.at[lane, pl.ds(places[lane] // size * size, size)]
        copy = pltpu.make_async_remote_copy(
            src_ref=held,
            dst_ref=held,
            send_sem=send_sem.at[lane, stage],
            recv_sem=recv_sem.at[lane, stage],
            device_id=(partner_of(me, orders[lane][bits - 1 - stage]),),
            device_id_type=pl.DeviceIdType.MESH,
        )
        copy.start()
        return copy

    def hand_over(lane, stage):
        size = 1 if stage == 0 else 2 ** (stage - 1)
        first = places[lane] // size
        if stage > 0:
            first = first + 1 - 2 * (first % 2)
        held = all_ref.at[lane, pl.ds(first * size, size)]
        copy = pltpu.make_async_remote_copy(
            src_ref=held,
            dst_ref=held,
            send_sem=hand_send.at[lane, stage],
            recv_sem=hand_recv.at[lane, stage],
            device_id=(partner_of(me, 0),),
            device_id_type=pl.DeviceIdType.MESH,
        )
        copy.start()
        return copy

    flying = []
    handed = []
    for lane in range(2):
        own[lane].wait()
        flying.append(start(lane, 0))
        handed.append(hand_over(lane, 0))
    for stage in range(1, bits):
        for lane in range(2):
            flying[lane].wait()
            if stage < bits - 1:
                flying[lane] = start(lane, stage)
            handed.append(hand_over(lane, stage))
    for copy in handed:
        copy.wait()


def gather(mine, count):
    lanes, half, width = mine.shape
    bits = count.bit_length() - 1
    return pl.pallas_call(
        partial(gather_kernel, count),
        in_specs=[pl.BlockSpec(memory_space=pltpu.VMEM)],
        out_specs=pl.BlockSpec(memory_space=pltpu.VMEM),
        out_shape=jax.ShapeDtypeStruct((lanes, count, half, width), mine.dtype),
        scratch_shapes=[
            pltpu.SemaphoreType.DMA((2,)),
            pltpu.SemaphoreType.DMA((2, bits)),
            pltpu.SemaphoreType.DMA((2, bits)),
            pltpu.SemaphoreType.DMA((2, bits)),
            pltpu.SemaphoreType.DMA((2, bits)),
        ],
        compiler_params=pltpu.CompilerParams(
            collective_id=0, has_side_effects=True, vmem_limit_bytes=40 * 1024 * 1024
        ),
    )(mine)


def reduce_kernel(count, all_ref, sum_ref, land_ref, send_sem, recv_sem):
    me = lax.axis_index("dp")
    orders = bit_orders(count)
    bits = len(orders[0])
    places = [place_of(me, order) for order in orders]
    greet(me, bits)

    def start(lane, stage):
        size = count // 2 ** (stage + 1)
        side = places[lane] // size % 2
        source = land_ref.at[lane, pl.ds(2 * size + (1 - side) * size, size)]
        copy = pltpu.make_async_remote_copy(
            src_ref=source,
            dst_ref=land_ref.at[lane, pl.ds(size, size)],
            send_sem=send_sem.at[lane, stage],
            recv_sem=recv_sem.at[lane, stage],
            device_id=(partner_of(me, orders[lane][stage]),),
            device_id_type=pl.DeviceIdType.MESH,
        )
        copy.start()
        return copy

    def add(lane, stage):
        size = count // 2 ** (stage + 1)
        side = places[lane] // size % 2

        def one(block):
            kept = land_ref[lane, 2 * size + side * size + block]
            return kept.astype(F32) + land_ref[lane, size + block].astype(F32)

        if stage == bits - 1:
            sum_ref[lane] = one(0)
        else:

            def body(block, carry):
                land_ref[lane, size + block] = one(block).astype(BF16)
                return carry

            lax.fori_loop(0, size, body, 0)

    quarter = count // 4

    def first_place(lane, piece):
        side = places[lane] // quarter % 2
        return (1 - side if piece == 0 else side) * quarter

    def first_start(lane, piece):
        side = places[lane] // (2 * quarter) % 2
        offset = first_place(lane, piece)
        copy = pltpu.make_async_remote_copy(
            src_ref=all_ref.at[lane, pl.ds((1 - side) * 2 * quarter + offset, quarter)],
            dst_ref=land_ref.at[lane, pl.ds(2 * quarter + offset, quarter)],
            send_sem=send_sem.at[lane, piece * bits],
            recv_sem=recv_sem.at[lane, piece * bits],
            device_id=(partner_of(me, orders[lane][0]),),
            device_id_type=pl.DeviceIdType.MESH,
        )
        copy.start()
        return copy

    def first_add(lane, piece):
        side = places[lane] // (2 * quarter) % 2
        offset = first_place(lane, piece)

        def body(block, carry):
            kept = all_ref[lane, side * 2 * quarter + offset + block].astype(F32)
            there = 2 * quarter + offset + block
            land_ref[lane, there] = (kept + land_ref[lane, there].astype(F32)).astype(BF16)
            return carry

        lax.fori_loop(0, quarter, body, 0)

    opening = [[first_start(lane, piece) for lane in range(2)] for piece in range(2)]
    flying = [None, None]
    for lane in range(2):
        opening[0][lane].wait()
        first_add(lane, 0)
        flying[lane] = start(lane, 1)
    for lane in range(2):
        opening[1][lane].wait()
        first_add(lane, 1)
    for stage in range(1, bits):
        for lane in range(2):
            flying[lane].wait()
            add(lane, stage)
            if stage < bits - 1:
                flying[lane] = start(lane, stage + 1)


def reduce(parts):
    lanes, count, half, width = parts.shape
    bits = count.bit_length() - 1
    return pl.pallas_call(
        partial(reduce_kernel, count),
        in_specs=[pl.BlockSpec(memory_space=pltpu.VMEM)],
        out_specs=pl.BlockSpec(memory_space=pltpu.VMEM),
        out_shape=jax.ShapeDtypeStruct((lanes, half, width), F32),
        scratch_shapes=[
            pltpu.VMEM((lanes, count, half, width), BF16),
            pltpu.SemaphoreType.DMA((2, bits + 1)),
            pltpu.SemaphoreType.DMA((2, bits + 1)),
        ],
        compiler_params=pltpu.CompilerParams(
            collective_id=1, has_side_effects=True, vmem_limit_bytes=40 * 1024 * 1024
        ),
    )(parts)


def dot(a, b):
    return jnp.dot(a, b, preferred_element_type=F32)


def dot_nt(a, b):
    return lax.dot_general(a, b, (((1,), (1,)), ((), ())), preferred_element_type=F32)


def dot_tn(a, b):
    return lax.dot_general(a, b, (((0,), (0,)), ((), ())), preferred_element_type=F32)


def load_piece(flat, name, column):
    start, rows, width = PLACE[name]
    if rows == 1:
        return flat[start + column : start + column + 1, :]
    return flat[pl.ds(start + column, rows, stride=width), :]


def store_piece(flat, name, column, value):
    start, rows, width = PLACE[name]
    if rows == 1:
        flat[start + column : start + column + 1, :] = value
    else:
        flat[pl.ds(start + column, rows, stride=width), :] = value


def layer_norm(values):
    average = jnp.mean(values, axis=-1, keepdims=True)
    centered = values - average
    inv_std = lax.rsqrt(jnp.mean(centered * centered, axis=-1, keepdims=True) + 1e-06)
    return centered * inv_std, inv_std


def norm_back(grad, normed, inv_std):
    mean_grad = jnp.mean(grad, axis=-1, keepdims=True)
    mean_proj = jnp.mean(grad * normed, axis=-1, keepdims=True)
    return inv_std * (grad - mean_grad - normed * mean_proj)


def column_sum(values):
    return jnp.sum(values, axis=0, keepdims=True)


def block_kernel(
    steps,
    rows,
    lat_ref,
    cot_ref,
    cond_ref,
    par_ref,
    out_ref,
    glat_ref,
    gcond_ref,
    gpar_ref,
    flat_ref,
    ada_w,
    qkv_w,
    out_w,
    fc1_w,
    fc2_w,
    qkv_t,
    out_t,
    fc1_t,
    fc2_t,
    biases,
    mod_ref,
    gmod_ref,
    d_qkv,
    d_out,
    d_fc1,
    d_fc2t,
    d_qkvb,
    d_outb,
    d_fc1b,
    d_fc2b,
):
    step = pl.program_id(0)
    owners, half_rows = par_ref.shape[1:3]
    tall = owners * rows
    orders = bit_orders(owners)
    spans = ((0, half_rows), (half_rows, rows))

    @pl.when(step == 0)
    def _():
        for owner in range(owners):
            for lane, (first, last) in enumerate(spans):
                flat_ref[owner * rows + first : owner * rows + last, :] = par_ref[
                    lane, place_of(owner, orders[lane])
                ].astype(F32)[: last - first]
        for name, ref in (
            ("ada_w", ada_w),
            ("qkv_w", qkv_w),
            ("out_w", out_w),
            ("fc1_w", fc1_w),
            ("fc2_w", fc2_w),
        ):
            for column in range(PLACE[name][2]):
                ref[:, column * LANE : (column + 1) * LANE] = load_piece(
                    flat_ref, name, column
                ).astype(BF16)
        qkv_t[...] = qkv_w[...].T
        out_t[...] = out_w[...].T
        fc1_t[...] = fc1_w[...].T
        fc2_t[...] = fc2_w[...].T
        biases[...] = jnp.zeros_like(biases)
        for row, (name, first) in enumerate(
            (("ada_b", 0), ("q_b", 0), ("v_b", 2 * D), ("out_b", 0), ("fc1_b", 0), ("fc2_b", 0))
        ):
            row = (0, 1, 1, 2, 3, 4)[row]
            for column in range(PLACE[name][2]):
                left = first + column * LANE
                biases[row : row + 1, left : left + LANE] = load_piece(flat_ref, name, column)
        cond = cond_ref[...]
        silu = (cond * jax.nn.sigmoid(cond)).astype(BF16)
        mod_ref[...] = dot(silu, ada_w[...]) + biases[0:1, :]
        for ref in (d_qkv, d_out, d_fc1, d_fc2t, d_qkvb, d_outb, d_fc1b, d_fc2b):
            ref[...] = jnp.zeros_like(ref)

    each = range(PER)
    mods = [mod_ref[pl.ds(step * PER + n, 1), :] for n in each]
    shift_a, scale_a, gate_a, shift_m, scale_m, gate_m = [
        [mods[n][:, piece * D : (piece + 1) * D] for n in each] for piece in range(6)
    ]

    def join(parts):
        return jnp.concatenate(parts, axis=0)

    def cut(values):
        return [values[n * SEQ : (n + 1) * SEQ] for n in each]

    low_half = lax.broadcasted_iota(jnp.int32, (SEQ, LANE), 1) < HEAD_DIM
    zero = jnp.zeros((SEQ, LANE), BF16)

    def half(values, head):
        return jnp.where(low_half, values, zero) if head % 2 == 0 else jnp.where(low_half, zero, values)

    def pair(values, head):
        left = head // 2 * LANE
        return values[:, left : left + LANE]

    x = [lat_ref[n].astype(F32) for n in each]
    cot = [cot_ref[n].astype(F32) for n in each]
    normed_a, inv_a = zip(*[layer_norm(x[n]) for n in each])
    hidden_a = join(
        [(normed_a[n] * (1.0 + scale_a[n]) + shift_a[n]).astype(BF16) for n in each]
    )
    qkv = (dot(hidden_a, qkv_w[...]) + biases[1:2, : 3 * D]).astype(BF16)
    query = cut(qkv[:, :D] * BF16(HEAD_DIM**-0.5))
    key = cut(qkv[:, D : 2 * D])
    value = cut(qkv[:, 2 * D :])
    key_t = [key[n].T * BF16(HEAD_DIM**-0.5) for n in each]
    value_t = [value[n].T for n in each]
    probs = [[] for n in each]
    probs_b = [[] for n in each]
    ctx_rows = [[] for n in each]
    for head in range(HEADS):
        head_rows = slice(head * HEAD_DIM, (head + 1) * HEAD_DIM)
        for n in each:
            scores = dot_nt(half(pair(key[n], head), head), pair(query[n], head)) * LOG2E
            grown = jnp.exp2(scores - jnp.max(scores, axis=0, keepdims=True))
            prob = grown * (1.0 / column_sum(grown))
            prob_b = prob.astype(BF16)
            probs[n].append(prob)
            probs_b[n].append(prob_b)
            ctx_rows[n].append(dot(value_t[n][head_rows, :], prob_b).astype(BF16))
    ctx_t = jnp.concatenate([join(ctx_rows[n]) for n in each], axis=1)
    attended = cut(dot(ctx_t.T, out_w[...]) + biases[2:3, :D])
    resid = [x[n] + gate_a[n] * attended[n] for n in each]
    normed_m, inv_m = zip(*[layer_norm(resid[n]) for n in each])
    hidden_m = join(
        [(normed_m[n] * (1.0 + scale_m[n]) + shift_m[n]).astype(BF16) for n in each]
    )
    hidden_mt = hidden_m.T
    g_mlp = join([(cot[n] * gate_m[n]).astype(BF16) for n in each])
    g_mlpt = g_mlp.T
    d_fc2b[...] += column_sum(g_mlp.astype(F32))
    mlp_out = biases[4:5, :D]
    g_hidden_m = None
    for left in range(0, FF, CHUNK):
        cols = slice(left, left + CHUNK)
        pre = dot(hidden_m, fc1_w[:, cols]) + biases[3:4, cols]
        square = pre * pre
        gate = 0.5 + 0.5 * jnp.tanh(pre * (GELU_C + (GELU_C * 0.044715) * square))
        act = pre * gate
        slope = gate + act * (1.0 - gate) * (2.0 * GELU_C + (6.0 * GELU_C * 0.044715) * square)
        act_b = act.astype(BF16)
        mlp_out = mlp_out + dot(act_b, fc2_w[cols, :])
        g_pre = dot(g_mlp, fc2_t[:, cols]) * slope
        g_pre_b = g_pre.astype(BF16)
        part = dot(g_pre_b, fc1_t[cols, :])
        g_hidden_m = part if g_hidden_m is None else g_hidden_m + part
        d_fc2t[:, cols] += dot(g_mlpt, act_b)
        d_fc1[:, cols] += dot(hidden_mt, g_pre_b)
        d_fc1b[:, cols] += column_sum(g_pre_b.astype(F32))
    mlp_out = cut(mlp_out)
    g_hidden_m = cut(g_hidden_m)
    g_resid = []
    for n in each:
        out_ref[n] = (resid[n] + gate_m[n] * mlp_out[n]).astype(BF16)
        g_resid.append(
            cot[n] + norm_back(g_hidden_m[n] * (1.0 + scale_m[n]), normed_m[n], inv_m[n])
        )
    late_mod = [
        [
            column_sum(g_resid[n] * attended[n]),
            column_sum(g_hidden_m[n]),
            column_sum(g_hidden_m[n] * normed_m[n]),
            column_sum(cot[n] * mlp_out[n]),
        ]
        for n in each
    ]
    g_attn = join([(g_resid[n] * gate_a[n]).astype(BF16) for n in each])
    d_out[...] += dot(ctx_t, g_attn)
    d_outb[...] += column_sum(g_attn.astype(F32))
    g_ctx = cut(dot(g_attn, out_t[...]).astype(BF16))
    gq_rows = [[] for n in each]
    g_keys = [[] for n in each]
    g_values = [[] for n in each]
    even = [None for n in each]
    for head in range(HEADS):
        head_rows = slice(head * HEAD_DIM, (head + 1) * HEAD_DIM)
        for n in each:
            g_prob = dot_nt(half(pair(value[n], head), head), pair(g_ctx[n], head))
            prob = probs[n][head]
            g_score = (prob * (g_prob - column_sum(g_prob * prob))).astype(BF16)
            gq_rows[n].append(dot(key_t[n][head_rows, :], g_score).astype(BF16))
            g_key = dot(g_score, pair(query[n], head))
            g_value = dot(probs_b[n][head], pair(g_ctx[n], head))
            if head % 2 == 0:
                even[n] = (g_key, g_value)
            else:
                g_keys[n].append(jnp.where(low_half, even[n][0], g_key).astype(BF16))
                g_values[n].append(jnp.where(low_half, even[n][1], g_value).astype(BF16))
    g_qkv = join(
        [
            jnp.concatenate([join(gq_rows[n]).T] + g_keys[n] + g_values[n], axis=1)
            for n in each
        ]
    )
    d_qkv[...] += dot(hidden_a.T, g_qkv)
    d_qkvb[...] += column_sum(g_qkv.astype(F32))
    g_hidden_a = cut(dot(g_qkv, qkv_t[...]))
    for n in each:
        glat_ref[n] = (
            g_resid[n] + norm_back(g_hidden_a[n] * (1.0 + scale_a[n]), normed_a[n], inv_a[n])
        ).astype(BF16)
        gmod_ref[pl.ds(step * PER + n, 1), :] = jnp.concatenate(
            [column_sum(g_hidden_a[n]), column_sum(g_hidden_a[n] * normed_a[n])] + late_mod[n],
            axis=1,
        )

    @pl.when(step == steps - 1)
    def _():
        cond = cond_ref[...]
        sig = jax.nn.sigmoid(cond)
        silu = (cond * sig).astype(BF16)
        g_mod = gmod_ref[...].astype(BF16)
        gcond_ref[...] = dot_nt(g_mod, ada_w[...]) * (sig * (1.0 + cond * (1.0 - sig)))
        mod_sum = column_sum(g_mod.astype(F32))

        def put(name, value, first=0):
            for column in range(PLACE[name][2]):
                left = first + column * LANE
                store_piece(flat_ref, name, column, value[:, left : left + LANE])

        for column in range(0, 6 * D, D):
            part = dot_tn(silu, g_mod[:, column : column + D])
            for inner in range(D // LANE):
                store_piece(
                    flat_ref,
                    "ada_w",
                    column // LANE + inner,
                    part[:, inner * LANE : (inner + 1) * LANE],
                )
        put("ada_b", mod_sum)
        put("qkv_w", d_qkv)
        put("q_b", d_qkvb)
        put("v_b", d_qkvb, 2 * D)
        put("out_w", d_out)
        put("out_b", d_outb)
        put("fc1_w", d_fc1)
        put("fc1_b", d_fc1b)
        for column in range(D // LANE):
            store_piece(
                flat_ref, "fc2_w", column, d_fc2t[column * LANE : (column + 1) * LANE, :].T
            )
        put("fc2_b", d_fc2b)
        flat_ref[USED:tall, :] = jnp.zeros((tall - USED, LANE), F32)
        for owner in range(owners):
            for lane, (first, last) in enumerate(spans):
                block = flat_ref[owner * rows + first : owner * rows + last, :]
                if last - first < half_rows:
                    rest = jnp.zeros((half_rows - (last - first), LANE), F32)
                    block = jnp.concatenate([block, rest], axis=0)
                gpar_ref[lane, place_of(owner, orders[lane])] = block.astype(BF16)


def run_block(latents, cotangent, condition, flat, rows):
    count = latents.shape[0]
    once = pl.Buffered(1)
    latent_spec = pl.BlockSpec((PER, SEQ, D), lambda i: (i, 0, 0))
    return pl.pallas_call(
        partial(block_kernel, count // PER, rows),
        grid=(count // PER,),
        in_specs=[
            latent_spec,
            latent_spec,
            pl.BlockSpec((count, D), lambda i: (0, 0), pipeline_mode=once),
            pl.BlockSpec(flat.shape, lambda i: (0, 0, 0, 0), pipeline_mode=once),
        ],
        out_specs=[
            latent_spec,
            latent_spec,
            pl.BlockSpec((count, D), lambda i: (0, 0), pipeline_mode=once),
            pl.BlockSpec(flat.shape, lambda i: (0, 0, 0, 0), pipeline_mode=once),
        ],
        out_shape=[
            jax.ShapeDtypeStruct(latents.shape, BF16),
            jax.ShapeDtypeStruct(latents.shape, BF16),
            jax.ShapeDtypeStruct((count, D), F32),
            jax.ShapeDtypeStruct(flat.shape, BF16),
        ],
        scratch_shapes=[
            pltpu.VMEM((flat.shape[1] * rows, LANE), F32),
            pltpu.VMEM((D, 6 * D), BF16),
            pltpu.VMEM((D, 3 * D), BF16),
            pltpu.VMEM((D, D), BF16),
            pltpu.VMEM((D, FF), BF16),
            pltpu.VMEM((FF, D), BF16),
            pltpu.VMEM((3 * D, D), BF16),
            pltpu.VMEM((D, D), BF16),
            pltpu.VMEM((FF, D), BF16),
            pltpu.VMEM((D, FF), BF16),
            pltpu.VMEM((8, 6 * D), F32),
            pltpu.VMEM((count, 6 * D), F32),
            pltpu.VMEM((count, 6 * D), F32),
            pltpu.VMEM((D, 3 * D), F32),
            pltpu.VMEM((D, D), F32),
            pltpu.VMEM((D, FF), F32),
            pltpu.VMEM((D, FF), F32),
            pltpu.VMEM((1, 3 * D), F32),
            pltpu.VMEM((1, D), F32),
            pltpu.VMEM((1, FF), F32),
            pltpu.VMEM((1, D), F32),
        ],
        compiler_params=pltpu.CompilerParams(
            dimension_semantics=("arbitrary",), vmem_limit_bytes=60 * 1024 * 1024
        ),
    )(latents, cotangent, condition, flat)


def on_device(latents_in, class_ids, step_ids, class_table, step_table, params, cotangent):
    devices = lax.axis_size("dp")
    rows = params.shape[0] // LANE
    half_rows = -(-rows // 32) * 16
    mine = jnp.pad(params.reshape(rows, LANE), ((0, 2 * half_rows - rows), (0, 0)))
    flat = gather(mine.reshape(2, half_rows, LANE), devices)
    class_hot = (
        class_ids[:, None] == jnp.arange(class_table.shape[0], dtype=jnp.int32)[None, :]
    ).astype(BF16)
    step_hot = (
        step_ids[:, None] == jnp.arange(step_table.shape[0], dtype=jnp.int32)[None, :]
    ).astype(BF16)
    condition = dot(class_hot, class_table) + dot(step_hot, step_table)
    block_out, grad_latents, grad_condition, grad_flat = run_block(
        latents_in, cotangent, condition, flat, rows
    )
    grad_params = reduce(grad_flat).reshape(2 * half_rows, LANE)[:rows]
    return block_out, grad_latents, grad_condition, grad_params.reshape(-1)


def solution(mesh):
    in_specs = (P("dp", None, None), P("dp"), P("dp"), P(), P(), P("dp"), P("dp", None, None))
    out_specs = (P("dp", None, None), P("dp", None, None), P("dp", None), P("dp"))
    return jax.shard_map(
        on_device, mesh=mesh, in_specs=in_specs, out_specs=out_specs, check_vma=False
    )
```
